32 devices in a mesh: dp: 2 (over x), row: 4 (over y, core), col: 4 (over z).
Axes of the slice: x: 2, y: 2, z: 4, core: 2. Of those that a mesh axis runs over, the one named last changes fastest.
Arguments:
- layer_input: bfloat16 [32768, 1024], P(('dp', 'col'), 'row'), may hold values from -6 to 6
- gain_one: float32 [1024], P('row'), may hold values from 0.5 to 1.5
- gain_two: float32 [1024], P('row'), may hold values from 0.5 to 1.5
- query_key_value_weight: bfloat16 [1024, 3, 1024], P('row', None, 'col'), may hold values from -0.1875 to 0.1875
- w_out: bfloat16 [1024, 1024], P('col', 'row'), may hold values from -3.5 to 3.5
- w_in: bfloat16 [1024, 2, 2624], P('row', None, 'col'), may hold values from -0.1875 to 0.1875
- w_down: bfloat16 [2624, 1024], P('col', 'row'), may hold values from -0.125 to 0.125
- cotangent: bfloat16 [32768, 1024], P(('dp', 'col'), 'row'), may hold values from -6 to 6
Outputs:
- output: bfloat16 [32768, 1024], P(('dp', 'col'), 'row')
- grad_input: bfloat16 [32768, 1024], P(('dp', 'col'), 'row')
- grad_w_qkv: float32 [1024, 3, 1024], P('row', None, 'col')
- grad_w_out: float32 [1024, 1024], P('col', 'row')
- grad_w_in: float32 [1024, 2, 2624], P('row', None, 'col')
- grad_w_down: float32 [2624, 1024], P('col', 'row')
- grad_gain_one: float32 [1024], P('row')
- grad_gain_two: float32 [1024], P('row')
The draws below stay inside these ranges and needn't reach their ends.
All inputs are finite; a program needn't handle non-finite values.
Results may differ from the reference program's by a relative error of at most 0.015.
Values may be sent and summed in bfloat16 or wider, within the bound.
A program may use at most 384 MiB of HBM per device.

```python
import math
import jax
import jax.numpy as jnp
from jax import lax

D = 1024
HEADS = 16
HD = 64
FF = 2624
LEN = 1024
TOKENS = 32768


def shard_levels(rng, extent, cuts, least, top_value):
    loudness, own = 1.0, jax.random.fold_in(rng, 6)
    for axis_at, blocks in cuts:
        draws = jnp.exp(jax.random.uniform(jax.random.fold_in(own, axis_at), (blocks,), jnp.float32, least / len(cuts), top_value / len(cuts)))
        loudness = loudness * jnp.repeat(draws, extent[axis_at] // blocks).reshape([-1 if axis == axis_at else 1 for axis in range(len(extent))])
    return loudness


def centred(rng, dims, width, most, split=(), held_as=jnp.bfloat16):
    values = jax.random.normal(rng, dims, jnp.float32) * width
    if len(split) > 0:
        values = shard_levels(rng, dims, split, -0.22, 0.18) * values
    return jnp.clip(values, min=-most, max=most).astype(held_as)


def setup_inputs(seed: int = 0) -> dict:
    splits = jax.random.split(jax.random.key(seed), 9)
    layer_input = centred(splits[0], (TOKENS, D), 1.0, 6.0, ((0, 8), (1, 4)))
    gain_one = jnp.clip(1.0 + 0.1 * jax.random.normal(splits[1], (D,), jnp.float32), 0.5, 1.5)
    gain_two = jnp.clip(1.0 + 0.1 * jax.random.normal(splits[2], (D,), jnp.float32), 0.5, 1.5)
    query_key_value_weight = centred(splits[3], (D, 3, D), D ** -0.5, 0.1875, ((0, 4), (2, 4)))
    w_out = centred(splits[4], (D, D), (max(1, 3 * D // LEN)) ** -0.5, 3.5, ((0, 4), (1, 4)))
    w_in = centred(splits[5], (D, 2, FF), D ** -0.5, 0.1875, ((0, 4), (2, 4)))
    w_down = centred(splits[6], (FF, D), FF ** -0.5, 0.125, ((0, 4), (1, 4)))
    cotangent = centred(splits[7], (TOKENS, D), 1.0, 6.0, ((0, 8), (1, 4)))
    return dict(layer_input=layer_input, gain_one=gain_one, gain_two=gain_two, query_key_value_weight=query_key_value_weight, w_out=w_out, w_in=w_in, w_down=w_down, cotangent=cotangent)


@jax.custom_vjp
def low(v):
    return lax.optimization_barrier(v.astype(jnp.bfloat16)).astype(jnp.float32)

@jax.custom_vjp
def reduced_precision_backward(v):
    return v

def low_keep(v):
    return (low(v), None)

def low_pass(kept, grad):
    return (grad,)

def back_keep(v):
    return (v, None)

def back_low(kept, grad):
    return (low(grad),)
low.defvjp(low_keep, low_pass)
reduced_precision_backward.defvjp(back_keep, back_low)
MATMUL_ACCURACY = lax.Precision.HIGHEST

def layer_norm(values, gain):
    mean = lax.optimization_barrier(jnp.mean(values, axis=-1, keepdims=True))
    square = lax.optimization_barrier(jnp.mean(values * values, axis=-1, keepdims=True))
    return (values - mean) * lax.rsqrt(square - mean * mean + 1e-05) * gain

def angles(length, size):
    inverse = 160000.0 ** (-jnp.arange(0, size, 2, dtype=jnp.float32) / size)
    phase = jnp.arange(length, dtype=jnp.float32)[:, None] * inverse[None, :]
    phase = jnp.concatenate([phase, phase], axis=-1)[:, None, :]
    return (jnp.cos(phase), jnp.sin(phase))

def rotate(values, cosine, sine):
    half = values.shape[-1] // 2
    turned = jnp.concatenate([-values[..., half:], values[..., :half]], axis=-1)
    return values * cosine + turned * sine

def attend(query, key, value):
    scale = HD ** (-0.5)
    block = math.gcd(LEN, 512)

    def one_block(query_block):
        scores = reduced_precision_backward(jnp.einsum('qhd,khd->hqk', query_block, key, precision=MATMUL_ACCURACY) * scale)
        probs = jax.nn.softmax(scores, axis=-1)
        return jnp.einsum('hqk,khd->qhd', low(probs), value, precision=MATMUL_ACCURACY)
    blocks = query.reshape(LEN // block, block, HEADS, HD)
    result = lax.map(jax.checkpoint(one_block), blocks)
    return result.reshape(LEN, HEADS, HD)

def layer(values, gain_one, gain_two, query_key_value_weight, w_out, w_in, w_down):
    cosine, sine = angles(LEN, HD)
    first_normalized = low(layer_norm(values, gain_one))
    attention_projected = reduced_precision_backward(jnp.einsum('nq,qac->nac', first_normalized, query_key_value_weight, precision=MATMUL_ACCURACY))
    attention_projected = attention_projected.reshape(LEN, 3, HEADS, HD)
    query = low(rotate(attention_projected[:, 0], cosine, sine))
    key = low(rotate(attention_projected[:, 1], cosine, sine))
    value = low(attention_projected[:, 2])
    mixed = attend(query, key, value).reshape(LEN, D)
    mixed = low(reduced_precision_backward(mixed))
    middle = values + reduced_precision_backward(jnp.dot(mixed, w_out, precision=MATMUL_ACCURACY))
    second_normalized = low(layer_norm(middle, gain_two))
    gate_up_output = reduced_precision_backward(jnp.einsum('td,dsf->tsf', second_normalized, w_in, precision=MATMUL_ACCURACY))
    hidden = low(jax.nn.gelu(gate_up_output[:, 0], approximate=False) * gate_up_output[:, 1])
    return middle + reduced_precision_backward(jnp.dot(hidden, w_down, precision=MATMUL_ACCURACY))

def reference(layer_input, gain_one, gain_two, query_key_value_weight, w_out, w_in, w_down, cotangent):
    params = tuple((a.astype(jnp.float32) for a in (gain_one, gain_two, query_key_value_weight, w_out, w_in, w_down)))
    seq_input = layer_input.astype(jnp.float32).reshape(-1, LEN, D)
    seq_grad = cotangent.astype(jnp.float32).reshape(-1, LEN, D)

    def step(totals, item):
        values, grads_out = item
        result, pull = jax.vjp(layer, values, *params)
        grads = pull(grads_out)
        totals = tuple((t + g for t, g in zip(totals, grads[1:])))
        return (totals, (result, grads[0]))
    zeros = tuple((jnp.zeros_like(p) for p in params))
    totals, (results, grads_in) = lax.scan(step, zeros, (seq_input, seq_grad))
    output = results.reshape(TOKENS, D).astype(jnp.bfloat16)
    grad_input = grads_in.reshape(TOKENS, D).astype(jnp.bfloat16)
    return (output, grad_input, totals[2], totals[3], totals[4], totals[5], totals[0], totals[1])
```

```python
import functools

import jax
import jax.numpy as jnp
from jax import lax
from jax.experimental import pallas as pl
from jax.experimental.pallas import tpu as pltpu
from jax.sharding import PartitionSpec as P

HD = 64
LEN = 1024
PAIR = 2 * HD
CHUNK = 512

EPSILON = 1e-05
THETA = 160000.0
BOTH = ("col", "row")
VMEM = 56 * 1024 * 1024


def turning(size):
    positions = jnp.arange(LEN).astype(jnp.float32)
    inverse = THETA ** (-jnp.arange(0, size, 2, dtype=jnp.float32) / size)
    phase = positions[:, None] * inverse[None, :]
    phase = jnp.concatenate([phase] * (2 * PAIR // size), axis=-1)
    return (jnp.cos(phase), jnp.sin(phase))


def first_half(shape):
    lane = lax.broadcasted_iota(jnp.int32, shape, len(shape) - 1)
    return lane % HD < HD // 2


def turn(values):
    ahead = pltpu.roll(values, PAIR - HD // 2, 1)
    behind = pltpu.roll(values, HD // 2, 1)
    return jnp.where(first_half(values.shape), -ahead, behind)


def unturn(values):
    ahead = pltpu.roll(values, PAIR - HD // 2, 1)
    behind = pltpu.roll(values, HD // 2, 1)
    return jnp.where(first_half(values.shape), ahead, -behind)


def dot(left, right, over):
    return lax.dot_general(left, right, (over, ((), ())), preferred_element_type=jnp.float32)


def attend_kernel(q_ref, k_ref, v_ref, cos_ref, sin_ref, qo_ref, ko_ref, vo_ref, mixed_ref):
    cosine, sine = cos_ref[...], sin_ref[...]
    query = q_ref[0]
    query = (query * cosine + turn(query) * sine).astype(jnp.bfloat16)
    key = k_ref[0]
    key = (key * cosine + turn(key) * sine).astype(jnp.bfloat16)
    value = v_ref[0].astype(jnp.bfloat16)
    qo_ref[...] = query
    ko_ref[...] = key
    vo_ref[...] = value
    scale = HD ** (-0.5)
    for start in range(0, LEN, CHUNK):
        parts = []
        for head in range(2):
            lanes = slice(head * HD, head * HD + HD)
            scores = dot(query[start : start + CHUNK, lanes], key[:, lanes], ((1,), (1,)))
            top = jnp.max(scores, axis=-1, keepdims=True)
            exponent = jnp.exp((scores - top) * scale)
            total = jnp.sum(exponent, axis=-1, keepdims=True)
            part = dot(exponent.astype(jnp.bfloat16), value[:, lanes], ((1,), (0,)))
            parts.append(part / total)
        mixed_ref[start : start + CHUNK, :] = jnp.concatenate(parts, axis=1).astype(jnp.bfloat16)


def attend_back_kernel(q_ref, k_ref, v_ref, do_ref, cos_ref, sin_ref, dq_ref, dk_ref, dv_ref):
    scale = HD ** (-0.5)
    dqs, dks, dvs = [], [], []
    for head in range(2):
        lanes = slice(head * HD, head * HD + HD)
        key = k_ref[:, lanes]
        value = v_ref[:, lanes]
        dq_parts, dk, dv = [], None, None
        for start in range(0, LEN, CHUNK):
            query = q_ref[start : start + CHUNK, lanes]
            grad = do_ref[start : start + CHUNK, lanes]
            scores = dot(key, query, ((1,), (1,)))
            top = jnp.max(scores, axis=0, keepdims=True)
            exponent = jnp.exp((scores - top) * scale)
            probs = exponent * (1.0 / jnp.sum(exponent, axis=0, keepdims=True))
            value_part = dot(probs.astype(jnp.bfloat16), grad, ((1,), (0,)))
            grad_probs = dot(value, grad, ((1,), (1,)))
            inner = jnp.sum(probs * grad_probs, axis=0, keepdims=True)
            grad_scores = (probs * (grad_probs - inner)).astype(jnp.bfloat16)
            key_part = dot(grad_scores, query, ((1,), (0,)))
            dq_parts.append(dot(grad_scores, key, ((0,), (0,))))
            dk = key_part if dk is None else dk + key_part
            dv = value_part if dv is None else dv + value_part
        dqs.append(jnp.concatenate(dq_parts, axis=0))
        dks.append(dk)
        dvs.append(dv)
    cosine, sine = cos_ref[...], sin_ref[...]
    dq = jnp.concatenate(dqs, axis=1) * scale
    dk = jnp.concatenate(dks, axis=1) * scale
    dq_ref[0] = (dq * cosine + unturn(dq * sine)).astype(jnp.bfloat16)
    dk_ref[0] = (dk * cosine + unturn(dk * sine)).astype(jnp.bfloat16)
    dv_ref[0] = jnp.concatenate(dvs, axis=1).astype(jnp.bfloat16)


def attend_forward(projected, cosine, sine):
    cols, rows, width = projected.shape
    pairs = width // 3 // PAIR

    def wide(which):
        return pl.BlockSpec(
            (1, LEN, PAIR), lambda s, c, p, which=which: (c, s, which * pairs + p)
        )

    angle = pl.BlockSpec((LEN, PAIR), lambda s, c, p: (0, 0))
    flat = pl.BlockSpec((LEN, PAIR), lambda s, c, p: (s, c * pairs + p))
    shape = jax.ShapeDtypeStruct((rows, cols * pairs * PAIR), jnp.bfloat16)
    return pl.pallas_call(
        attend_kernel,
        grid=(rows // LEN, cols, pairs),
        in_specs=[wide(0), wide(1), wide(2), angle, angle],
        out_specs=[flat] * 4,
        out_shape=[shape] * 4,
        compiler_params=pltpu.CompilerParams(vmem_limit_bytes=VMEM),
        name="attend_forward",
    )(projected, projected, projected, cosine, sine)


def attend_backward(query, key, value, grad_mixed, cosine, sine, cols):
    rows, width = query.shape
    pairs = width // cols // PAIR
    angle = pl.BlockSpec((LEN, PAIR), lambda s, c, p: (0, 0))
    flat = pl.BlockSpec((LEN, PAIR), lambda s, c, p: (s, c * pairs + p))
    out = pl.BlockSpec((1, LEN, PAIR), lambda s, c, p: (c, s, p))
    shape = jax.ShapeDtypeStruct((cols, rows, pairs * PAIR), jnp.bfloat16)
    parts = pl.pallas_call(
        attend_back_kernel,
        grid=(rows // LEN, cols, pairs),
        in_specs=[flat] * 4 + [angle] * 2,
        out_specs=[out] * 3,
        out_shape=[shape] * 3,
        compiler_params=pltpu.CompilerParams(vmem_limit_bytes=VMEM),
        name="attend_backward",
    )(query, key, value, grad_mixed, cosine, sine)
    return jnp.concatenate(parts, axis=2)


def norm_forward(values):
    mean = jnp.mean(values, axis=1, keepdims=True)
    square = jnp.mean(values * values, axis=1, keepdims=True)
    rstd = lax.rsqrt(square - mean * mean + EPSILON)
    return ((values - mean) * rstd, rstd)


def norm_backward(grads, centred, rstd, gain):
    scaled = grads * gain
    first = jnp.mean(scaled, axis=1, keepdims=True)
    second = jnp.mean(scaled * centred, axis=1, keepdims=True)
    result = rstd * (scaled - first - centred * second)
    return (result, jnp.sum(grads * centred, axis=0))


def gather(block):
    return lax.all_gather(block, BOTH, axis=0, tiled=False)


def scatter(blocks):
    return lax.psum_scatter(blocks.astype(jnp.bfloat16), BOTH, scatter_dimension=0, tiled=False)


def per_device(
    layer_input, gain_one, gain_two, query_key_value_weight, w_out, w_in, w_down, cotangent
):
    cols, rows_axis = lax.axis_size("col"), lax.axis_size("row")
    part = query_key_value_weight.shape[0]
    width = part * rows_axis
    hid = w_down.shape[0]
    f32, bf16 = jnp.float32, jnp.bfloat16

    residual_low = lax.all_to_all(layer_input, "row", 0, 1, tiled=True)
    gains = lax.all_gather(jnp.stack([gain_one, gain_two]), "row", axis=1, tiled=True)
    full_one, full_two = gains[0], gains[1]
    qkv = gather(query_key_value_weight.reshape(part, -1)).reshape(cols, width, -1)
    out = gather(w_out).reshape(cols, rows_axis, part, part)
    gate_w = gather(w_in[:, 0]).reshape(cols, width, hid)
    up_w = gather(w_in[:, 1]).reshape(cols, width, hid)
    down = gather(w_down).reshape(cols, rows_axis, hid, part)
    down = jnp.swapaxes(down, 1, 2).reshape(cols, hid, width)
    out = jnp.swapaxes(out, 1, 2).reshape(width, width)
    grad_out = lax.all_to_all(cotangent, "row", 0, 1, tiled=True)

    residual_in = residual_low.astype(f32)
    rows = residual_in.shape[0]
    cosine, sine = turning(HD)
    centred_one, rstd_one = norm_forward(residual_in)
    normed_one = (centred_one * full_one).astype(bf16)
    projected = jnp.einsum("td,cdn->ctn", normed_one, qkv, preferred_element_type=f32)
    query, key, value, mixed = attend_forward(projected, cosine, sine)
    middle = residual_in + jnp.dot(mixed, out, preferred_element_type=f32)
    centred_two, rstd_two = norm_forward(middle)
    normed_two = (centred_two * full_two).astype(bf16)
    gate = jnp.einsum("td,cdn->ctn", normed_two, gate_w, preferred_element_type=f32)
    up = jnp.einsum("td,cdn->ctn", normed_two, up_w, preferred_element_type=f32)
    hidden = (jax.nn.gelu(gate, approximate=False) * up).astype(bf16)
    output = middle + jnp.einsum("ctn,cnd->td", hidden, down, preferred_element_type=f32)
    output = lax.all_to_all(output.astype(bf16), "row", 1, 0, tiled=True)

    grad_hidden = jnp.einsum("td,cnd->ctn", grad_out, down, preferred_element_type=f32)
    grad_down = jnp.einsum("ctn,trd->crnd", hidden, grad_out.reshape(rows, rows_axis, part), preferred_element_type=f32)
    grad_down = scatter(grad_down.reshape(-1, hid, part))
    _, pull = jax.vjp(lambda g, u: jax.nn.gelu(g, approximate=False) * u, gate, up)
    grad_gate, grad_up = pull(grad_hidden)
    grad_gate, grad_up = grad_gate.astype(bf16), grad_up.astype(bf16)
    grad_gate_w = jnp.einsum("td,ctn->cdn", normed_two, grad_gate, preferred_element_type=f32)
    grad_gate_w = scatter(grad_gate_w.reshape(-1, part, hid))
    grad_up_w = jnp.einsum("td,ctn->cdn", normed_two, grad_up, preferred_element_type=f32)
    grad_up_w = scatter(grad_up_w.reshape(-1, part, hid))
    grad_normed_two = jnp.einsum(
        "ctn,cdn->td", grad_gate, gate_w, preferred_element_type=f32
    ) + jnp.einsum("ctn,cdn->td", grad_up, up_w, preferred_element_type=f32)
    grad_norm_two, gain_part_two = norm_backward(grad_normed_two, centred_two, rstd_two, full_two)
    grad_middle = grad_out.astype(f32) + grad_norm_two
    branch = grad_middle.astype(bf16)
    grad_mixed = dot(branch, out, ((1,), (1,))).astype(bf16)
    grad_w_out = jnp.einsum(
        "tcm,trd->crmd",
        mixed.reshape(rows, cols, part),
        branch.reshape(rows, rows_axis, part),
        preferred_element_type=f32,
    )
    grad_w_out = scatter(grad_w_out.reshape(-1, part, part))
    grad_projected = attend_backward(query, key, value, grad_mixed, cosine, sine, cols)
    grad_normed_one = jnp.einsum("ctn,cdn->td", grad_projected, qkv, preferred_element_type=f32)
    grad_qkv = jnp.einsum("td,ctn->cdn", normed_one, grad_projected, preferred_element_type=f32)
    grad_qkv = scatter(grad_qkv.reshape(-1, part, qkv.shape[2]))
    grad_norm_one, gain_part_one = norm_backward(
        grad_normed_one, centred_one, rstd_one, full_one
    )
    grad_input = (grad_middle + grad_norm_one).astype(bf16)
    grad_input = lax.all_to_all(grad_input, "row", 1, 0, tiled=True)

    sums = lax.psum((grad_down, grad_gate_w, grad_up_w, grad_w_out, grad_qkv), "dp")
    grad_down, grad_gate_w, grad_up_w, grad_w_out, grad_qkv = (s.astype(f32) for s in sums)
    gain_sums = lax.psum(jnp.stack([gain_part_one, gain_part_two]), ("dp", "col", "row"))
    mine = lax.dynamic_slice_in_dim(gain_sums, lax.axis_index("row") * part, part, 1)
    return (
        output,
        grad_input,
        grad_qkv.reshape(query_key_value_weight.shape),
        grad_w_out,
        jnp.stack([grad_gate_w, grad_up_w], axis=1),
        grad_down,
        mine[0],
        mine[1],
    )


def solution(mesh):
    in_specs = (
        P(("dp", "col"), "row"),
        P("row"),
        P("row"),
        P("row", None, "col"),
        P("col", "row"),
        P("row", None, "col"),
        P("col", "row"),
        P(("dp", "col"), "row"),
    )
    out_specs = (
        P(("dp", "col"), "row"),
        P(("dp", "col"), "row"),
        P("row", None, "col"),
        P("col", "row"),
        P("row", None, "col"),
        P("col", "row"),
        P("row"),
        P("row"),
    )
    return jax.shard_map(
        per_device, mesh=mesh, in_specs=in_specs, out_specs=out_specs, check_vma=False
    )
```

```python
import functools

import jax
import jax.numpy as jnp
from jax import lax
from jax.experimental import pallas as pl
from jax.experimental.pallas import tpu as pltpu
from jax.sharding import PartitionSpec as P

HD = 64
LEN = 1024
PAIR = 2 * HD
CHUNK = 512

EPSILON = 1e-05
THETA = 160000.0
BOTH = ("col", "row")
VMEM = 56 * 1024 * 1024


def turning(size):
    positions = jnp.arange(LEN).astype(jnp.float32)
    inverse = THETA ** (-jnp.arange(0, size, 2, dtype=jnp.float32) / size)
    phase = positions[:, None] * inverse[None, :]
    phase = jnp.concatenate([phase] * (2 * PAIR // size), axis=-1)
    return (jnp.cos(phase), jnp.sin(phase))


def first_half(shape):
    lane = lax.broadcasted_iota(jnp.int32, shape, len(shape) - 1)
    return lane % HD < HD // 2


def turn(values):
    ahead = pltpu.roll(values, PAIR - HD // 2, 1)
    behind = pltpu.roll(values, HD // 2, 1)
    return jnp.where(first_half(values.shape), -ahead, behind)


def unturn(values):
    ahead = pltpu.roll(values, PAIR - HD // 2, 1)
    behind = pltpu.roll(values, HD // 2, 1)
    return jnp.where(first_half(values.shape), ahead, -behind)


def dot(left, right, over):
    return lax.dot_general(left, right, (over, ((), ())), preferred_element_type=jnp.float32)


def attend_kernel(q_ref, k_ref, v_ref, cos_ref, sin_ref, qo_ref, ko_ref, vo_ref, mixed_ref):
    cosine, sine = cos_ref[...], sin_ref[...]
    query = q_ref[0]
    query = (query * cosine + turn(query) * sine).astype(jnp.bfloat16)
    key = k_ref[0]
    key = (key * cosine + turn(key) * sine).astype(jnp.bfloat16)
    value = v_ref[0].astype(jnp.bfloat16)
    qo_ref[...] = query
    ko_ref[...] = key
    vo_ref[...] = value
    scale = HD ** (-0.5)
    for start in range(0, LEN, CHUNK):
        parts = []
        for head in range(2):
            lanes = slice(head * HD, head * HD + HD)
            scores = dot(query[start : start + CHUNK, lanes], key[:, lanes], ((1,), (1,)))
            top = jnp.max(scores, axis=-1, keepdims=True)
            exponent = jnp.exp((scores - top) * scale)
            total = jnp.sum(exponent, axis=-1, keepdims=True)
            part = dot(exponent.astype(jnp.bfloat16), value[:, lanes], ((1,), (0,)))
            parts.append(part / total)
        mixed_ref[start : start + CHUNK, :] = jnp.concatenate(parts, axis=1).astype(jnp.bfloat16)


def attend_back_kernel(q_ref, k_ref, v_ref, do_ref, cos_ref, sin_ref, dq_ref, dk_ref, dv_ref):
    scale = HD ** (-0.5)
    dqs, dks, dvs = [], [], []
    for head in range(2):
        lanes = slice(head * HD, head * HD + HD)
        key = k_ref[:, lanes]
        value = v_ref[:, lanes]
        dq_parts, dk, dv = [], None, None
        for start in range(0, LEN, CHUNK):
            query = q_ref[start : start + CHUNK, lanes]
            grad = do_ref[start : start + CHUNK, lanes]
            scores = dot(key, query, ((1,), (1,)))
            top = jnp.max(scores, axis=0, keepdims=True)
            exponent = jnp.exp((scores - top) * scale)
            probs = exponent * (1.0 / jnp.sum(exponent, axis=0, keepdims=True))
            value_part = dot(probs.astype(jnp.bfloat16), grad, ((1,), (0,)))
            grad_probs = dot(value, grad, ((1,), (1,)))
            inner = jnp.sum(probs * grad_probs, axis=0, keepdims=True)
            grad_scores = (probs * (grad_probs - inner)).astype(jnp.bfloat16)
            key_part = dot(grad_scores, query, ((1,), (0,)))
            dq_parts.append(dot(grad_scores, key, ((0,), (0,))))
            dk = key_part if dk is None else dk + key_part
            dv = value_part if dv is None else dv + value_part
        dqs.append(jnp.concatenate(dq_parts, axis=0))
        dks.append(dk)
        dvs.append(dv)
    cosine, sine = cos_ref[...], sin_ref[...]
    dq = jnp.concatenate(dqs, axis=1) * scale
    dk = jnp.concatenate(dks, axis=1) * scale
    dq_ref[0] = (dq * cosine + unturn(dq * sine)).astype(jnp.bfloat16)
    dk_ref[0] = (dk * cosine + unturn(dk * sine)).astype(jnp.bfloat16)
    dv_ref[0] = jnp.concatenate(dvs, axis=1).astype(jnp.bfloat16)


def attend_forward(projected, cosine, sine):
    cols, rows, width = projected.shape
    pairs = width // 3 // PAIR

    def wide(which):
        return pl.BlockSpec(
            (1, LEN, PAIR), lambda s, c, p, which=which: (c, s, which * pairs + p)
        )

    angle = pl.BlockSpec((LEN, PAIR), lambda s, c, p: (0, 0))
    flat = pl.BlockSpec((LEN, PAIR), lambda s, c, p: (s, c * pairs + p))
    shape = jax.ShapeDtypeStruct((rows, cols * pairs * PAIR), jnp.bfloat16)
    return pl.pallas_call(
        attend_kernel,
        grid=(rows // LEN, cols, pairs),
        in_specs=[wide(0), wide(1), wide(2), angle, angle],
        out_specs=[flat] * 4,
        out_shape=[shape] * 4,
        compiler_params=pltpu.CompilerParams(vmem_limit_bytes=VMEM),
        name="attend_forward",
    )(projected, projected, projected, cosine, sine)


def attend_backward(query, key, value, grad_mixed, cosine, sine, cols):
    rows, width = query.shape
    pairs = width // cols // PAIR
    angle = pl.BlockSpec((LEN, PAIR), lambda s, c, p: (0, 0))
    flat = pl.BlockSpec((LEN, PAIR), lambda s, c, p: (s, c * pairs + p))
    out = pl.BlockSpec((1, LEN, PAIR), lambda s, c, p: (c, s, p))
    shape = jax.ShapeDtypeStruct((cols, rows, pairs * PAIR), jnp.bfloat16)
    parts = pl.pallas_call(
        attend_back_kernel,
        grid=(rows // LEN, cols, pairs),
        in_specs=[flat] * 4 + [angle] * 2,
        out_specs=[out] * 3,
        out_shape=[shape] * 3,
        compiler_params=pltpu.CompilerParams(vmem_limit_bytes=VMEM),
        name="attend_backward",
    )(query, key, value, grad_mixed, cosine, sine)
    return jnp.concatenate(parts, axis=2)


def norm_forward(values):
    mean = jnp.mean(values, axis=1, keepdims=True)
    square = jnp.mean(values * values, axis=1, keepdims=True)
    rstd = lax.rsqrt(square - mean * mean + EPSILON)
    return ((values - mean) * rstd, rstd)


def norm_backward(grads, centred, rstd, gain):
    scaled = grads * gain
    first = jnp.mean(scaled, axis=1, keepdims=True)
    second = jnp.mean(scaled * centred, axis=1, keepdims=True)
    result = rstd * (scaled - first - centred * second)
    return (result, jnp.sum(grads * centred, axis=0))


def gather(block):
    return lax.all_gather(block, BOTH, axis=0, tiled=False)


def scatter(blocks):
    return lax.psum_scatter(blocks, BOTH, scatter_dimension=0, tiled=False)


def sum_data(part):
    if lax.axis_size("dp") == 2:
        other = lax.ppermute(part, "dp", [(0, 1), (1, 0)])
        return part.astype(jnp.float32) + other.astype(jnp.float32)
    return lax.psum(part, "dp").astype(jnp.float32)


def per_device(
    layer_input, gain_one, gain_two, query_key_value_weight, w_out, w_in, w_down, cotangent
):
    cols, rows_axis = lax.axis_size("col"), lax.axis_size("row")
    part = query_key_value_weight.shape[0]
    width = part * rows_axis
    hid = w_down.shape[0]
    f32, bf16 = jnp.float32, jnp.bfloat16

    first_pack = jnp.concatenate([query_key_value_weight.reshape(part, -1), w_out], axis=1)
    first = gather(first_pack)
    second_pack = jnp.concatenate(
        [jnp.transpose(w_in, (1, 2, 0)), w_down[None]], axis=0
    )
    residual_low = lax.all_to_all(layer_input, "row", 0, 1, tiled=True)
    gains = jnp.broadcast_to(jnp.stack([gain_one, gain_two])[None], (rows_axis, 2, part))
    gains = lax.all_to_all(gains, "row", 0, 0, tiled=True)
    gains = jnp.swapaxes(gains, 0, 1).reshape(2, width)
    full_one, full_two = gains[0], gains[1]
    first, second_pack = lax.optimization_barrier((first, second_pack))
    second = gather(second_pack)
    grad_out = lax.all_to_all(cotangent, "row", 0, 1, tiled=True)

    first = first.reshape(cols, width, -1)
    qkv = first[:, :, :-part]
    out = first[:, :, -part:].reshape(cols, rows_axis, part, part)
    out = jnp.swapaxes(out, 1, 2).reshape(width, width)

    residual_in = residual_low.astype(f32)
    rows = residual_in.shape[0]
    cosine, sine = turning(HD)
    centred_one, rstd_one = norm_forward(residual_in)
    normed_one = (centred_one * full_one).astype(bf16)
    projected = jnp.einsum("td,cdn->ctn", normed_one, qkv, preferred_element_type=f32)
    query, key, value, mixed = attend_forward(projected, cosine, sine)
    middle = residual_in + jnp.dot(mixed, out, preferred_element_type=f32)
    centred_two, rstd_two = norm_forward(middle)
    normed_two = (centred_two * full_two).astype(bf16)

    second = second.reshape(cols, rows_axis, 3, hid, part)
    second = jnp.transpose(second, (2, 0, 3, 1, 4)).reshape(3, cols * hid, width)
    gate_w, up_w, down = second[0], second[1], second[2]
    gate = dot(normed_two, gate_w, ((1,), (1,)))
    up = dot(normed_two, up_w, ((1,), (1,)))
    hidden = (jax.nn.gelu(gate, approximate=False) * up).astype(bf16)
    output = middle + dot(hidden, down, ((1,), (0,)))
    output = lax.all_to_all(output.astype(bf16), "row", 1, 0, tiled=True)

    grad_hidden = dot(grad_out, down, ((1,), (1,)))
    _, pull = jax.vjp(lambda g, u: jax.nn.gelu(g, approximate=False) * u, gate, up)
    grad_gate, grad_up = pull(grad_hidden)
    grad_gate, grad_up = grad_gate.astype(bf16), grad_up.astype(bf16)

    def blocks(grad):
        grad = grad.astype(bf16).reshape(cols, hid, rows_axis, part)
        return jnp.swapaxes(grad, 1, 2).reshape(-1, hid, part)

    grad_second = jnp.stack(
        [
            blocks(dot(grad_gate, normed_two, ((0,), (0,)))),
            blocks(dot(grad_up, normed_two, ((0,), (0,)))),
            blocks(dot(hidden, grad_out, ((0,), (0,)))),
        ],
        axis=1,
    )
    grad_second = scatter(grad_second)
    grad_normed_two = dot(grad_gate, gate_w, ((1,), (0,))) + dot(grad_up, up_w, ((1,), (0,)))
    grad_norm_two, gain_part_two = norm_backward(grad_normed_two, centred_two, rstd_two, full_two)
    grad_middle = grad_out.astype(f32) + grad_norm_two
    branch = grad_middle.astype(bf16)
    grad_mixed = dot(branch, out, ((1,), (1,))).astype(bf16)
    grad_w_out = dot(mixed, branch, ((0,), (0,))).astype(bf16)
    grad_w_out = grad_w_out.reshape(cols, part, rows_axis, part)
    grad_w_out = jnp.swapaxes(grad_w_out, 1, 2).reshape(-1, part, part)
    grad_projected = attend_backward(query, key, value, grad_mixed, cosine, sine, cols)
    grad_qkv = jnp.einsum("td,ctn->cdn", normed_one, grad_projected, preferred_element_type=f32)
    grad_qkv = grad_qkv.astype(bf16).reshape(cols * rows_axis, part, -1)
    grad_first = scatter(jnp.concatenate([grad_qkv, grad_w_out], axis=2))
    grad_normed_one = jnp.einsum("ctn,cdn->td", grad_projected, qkv, preferred_element_type=f32)
    grad_norm_one, gain_part_one = norm_backward(
        grad_normed_one, centred_one, rstd_one, full_one
    )
    grad_input = (grad_middle + grad_norm_one).astype(bf16)
    grad_input = lax.all_to_all(grad_input, "row", 1, 0, tiled=True)

    grad_second = sum_data(grad_second)
    grad_first = sum_data(grad_first)
    gain_sums = lax.psum(jnp.stack([gain_part_one, gain_part_two]), ("dp", "col", "row"))
    mine = lax.dynamic_slice_in_dim(gain_sums, lax.axis_index("row") * part, part, 1)
    return (
        output,
        grad_input,
        grad_first[:, :-part].reshape(query_key_value_weight.shape),
        grad_first[:, -part:],
        jnp.transpose(grad_second[:2], (2, 0, 1)),
        grad_second[2],
        mine[0],
        mine[1],
    )


def solution(mesh):
    in_specs = (
        P(("dp", "col"), "row"),
        P("row"),
        P("row"),
        P("row", None, "col"),
        P("col", "row"),
        P("row", None, "col"),
        P("col", "row"),
        P(("dp", "col"), "row"),
    )
    out_specs = (
        P(("dp", "col"), "row"),
        P(("dp", "col"), "row"),
        P("row", None, "col"),
        P("col", "row"),
        P("row", None, "col"),
        P("col", "row"),
        P("row"),
        P("row"),
    )
    return jax.shard_map(
        per_device, mesh=mesh, in_specs=in_specs, out_specs=out_specs, check_vma=False
    )
```
